32 devices in a mesh: depth: 4 (over y, x), scan: 8 (over z, core).
Axes of the slice: x: 2, y: 2, z: 4, core: 2. Of those that a mesh axis runs over, the one named last changes fastest.
Arguments:
- object_slice: bfloat16 [2, 4, 512, 2048], P(None, None, 'depth', 'scan'), may hold values from -4 to 4
- probe_field: bfloat16 [2, 512, 512], replicated, may hold values from -2 to 2
- offsets: int32 [16, 2], replicated, may hold values from 0 to 1536
- assignment: int32 [16], P('scan'), may hold values from 0 to 15, each once
- intensities: float32 [16, 512, 512], P('scan', 'depth'), may hold values from 0 to 3
Outputs:
- object_grad: float32 [2, 4, 512, 2048], P(None, None, 'depth', 'scan')
- probe_grad: float32 [2, 512, 512], P(None, 'depth')
The draws below stay inside these ranges and needn't reach their ends.
Inputs may be any that keep to these rules, and one draw needn't show every extreme that they name: `offsets`: each window lies inside the object window. `assignment`: every position stands in exactly one slot; slots s * 2 to s * 2 + 1 lie on index s of scan.
All inputs are finite; a program needn't handle non-finite values.
Results may differ from the reference program's by a relative error of at most 0.0003.
Values may be sent and summed in bfloat16 or wider, within the bound.
A program may use at most 64 MiB of HBM per device.

```python
import math
import jax
import jax.numpy as jnp
from jax import lax

P_SIZE = 512
S = 2048
NPOS = 16
CYC = 4


def set_ends(drawn, rng, smallest, top_value):
    longest = drawn.shape.index(max(drawn.shape))
    spots = []
    for shift in (0, 1):
        where = [jax.random.randint(jax.random.fold_in(rng, axis), (), 0, length) for axis, length in enumerate(drawn.shape)]
        where[longest] = (where[longest] + shift) % drawn.shape[longest]
        spots.append(tuple(where))
    return drawn.at[spots[0]].set(smallest).at[spots[1]].set(top_value)


def block_scale(key, extent, split, smallest, largest):
    def one(dim, blocks):
        heights = jax.random.uniform(jax.random.fold_in(jax.random.fold_in(key, 6), dim), (blocks,), jnp.float32, smallest / len(split), largest / len(split))
        return jnp.repeat(jnp.exp(heights), extent[dim] // blocks).reshape((-1,) + (1,) * (len(extent) - dim - 1))

    gain = one(*split[0])
    for cut in split[1:]:
        gain = gain * one(*cut)
    return gain


def noise(stream_key, dims, width, most, split=(), kind=jnp.bfloat16):
    factor_of = block_scale(stream_key, dims, split, -0.22, 0.18) if split else 1.0
    entries = jax.random.normal(stream_key, dims, jnp.float32) * width * factor_of
    return jnp.minimum(jnp.maximum(entries, -most), most).astype(kind)


def setup_inputs(seed: int = 0) -> dict:
    splits = jax.random.split(jax.random.key(seed), 6)
    object_slice = noise(splits[0], (2, CYC, P_SIZE, S), 1.0, 4.0, ((2, 4), (3, 8)))
    probe_field = noise(splits[1], (2, P_SIZE, P_SIZE), 0.5, 2.0)
    offsets = set_ends(jax.random.randint(splits[2], (NPOS, 2), 0, S - P_SIZE + 1), jax.random.fold_in(splits[2], 1), 0, S - P_SIZE).astype(jnp.int32)
    assignment = jax.random.permutation(splits[3], NPOS).astype(jnp.int32)
    intensities = jnp.clip(3.0 * jax.random.uniform(splits[4], (NPOS, P_SIZE, P_SIZE), jnp.float32) ** block_scale(splits[4], (NPOS, P_SIZE, P_SIZE), ((0, 8), (1, 4)), -0.2, 0.2), 0.0, 3.0)
    return dict(object_slice=object_slice, probe_field=probe_field, offsets=offsets, assignment=assignment, intensities=intensities)


fresnel_scale = 4

def dft_table(size):
    index = jnp.arange(size, dtype=jnp.int32)
    turns = index[:, None] * index[None, :] % size
    angle = 2.0 * math.pi / size * turns.astype(jnp.float32)
    norm = 1.0 / math.sqrt(size)
    return (jnp.cos(angle) * norm, -jnp.sin(angle) * norm)

def chirp_phase(index, size):
    centred = index - size // 2
    period = 2 * fresnel_scale * size
    phase = centred * centred % period
    angle = math.pi / (fresnel_scale * size) * phase.astype(jnp.float32)
    return (jnp.cos(angle), jnp.sin(angle))

def contract(form, left_side, right_side):
    return jnp.einsum(form, left_side, right_side, precision=lax.Precision.HIGHEST, preferred_element_type=jnp.float32)

def complex_mix(form, left_re, left_im, right_re, right_im):
    real_part = contract(form, left_re, right_re) - contract(form, left_im, right_im)
    imag_part = contract(form, left_re, right_im) + contract(form, left_im, right_re)
    return (real_part, imag_part)

def reference(object_slice, probe_field, offsets, assignment, intensities):
    image = object_slice.reshape(2, S, S)
    table_re, table_im = dft_table(P_SIZE)
    index = jnp.arange(P_SIZE, dtype=jnp.int32)
    row_cos, row_sin = chirp_phase(index, P_SIZE)
    chirp_re = row_cos[:, None] * row_cos[None, :] - row_sin[:, None] * row_sin[None, :]
    chirp_im = row_sin[:, None] * row_cos[None, :] + row_cos[:, None] * row_sin[None, :]
    probe_re = probe_field[0].astype(jnp.float32)
    probe_im = probe_field[1].astype(jnp.float32)

    def visit(carry, slot_index):
        grad_image, grad_probe = carry
        position = offsets[assignment[slot_index]]
        top_row = position[0].astype(jnp.int32)
        left_col = position[1].astype(jnp.int32)
        corner = (jnp.int32(0), top_row, left_col)
        window = lax.dynamic_slice(image, corner, (2, P_SIZE, P_SIZE)).astype(jnp.float32)
        obj_re, obj_im = (window[0], window[1])
        wave_re = probe_re * obj_re - probe_im * obj_im
        wave_im = probe_re * obj_im + probe_im * obj_re
        psi_re = wave_re * chirp_re - wave_im * chirp_im
        psi_im = wave_re * chirp_im + wave_im * chirp_re
        half_re, half_im = complex_mix('vk,jk->vj', table_re, table_im, psi_re, psi_im)
        far_re, far_im = complex_mix('vj,ju->vu', half_re, half_im, table_re, table_im)
        excess = far_re * far_re + far_im * far_im - intensities[slot_index]
        resid_re = excess * far_re
        resid_im = excess * far_im
        mid_re, mid_im = complex_mix('vu,uj->vj', resid_re, resid_im, table_re, -table_im)
        back_re, back_im = complex_mix('vk,vj->jk', table_re, -table_im, mid_re, mid_im)
        grad_re = back_re * chirp_re + back_im * chirp_im
        grad_im = back_im * chirp_re - back_re * chirp_im
        contrib = jnp.stack([probe_re * grad_re + probe_im * grad_im, probe_re * grad_im - probe_im * grad_re])
        current = lax.dynamic_slice(grad_image, corner, (2, P_SIZE, P_SIZE))
        grad_image = lax.dynamic_update_slice(grad_image, current + contrib, corner)
        term = jnp.stack([obj_re * grad_re + obj_im * grad_im, obj_re * grad_im - obj_im * grad_re])
        return ((grad_image, grad_probe + term), None)
    start = (jnp.zeros((2, S, S), jnp.float32), jnp.zeros((2, P_SIZE, P_SIZE), jnp.float32))
    (grad_image, grad_probe), _ = lax.scan(visit, start, jnp.arange(NPOS, dtype=jnp.int32))
    return (grad_image.reshape(2, CYC, P_SIZE, S), grad_probe * NPOS ** (-0.5))
```

```python
import functools
import math

import jax
import jax.numpy as jnp
import ml_dtypes
import numpy as np
from jax import lax
from jax.experimental import pallas as pl
from jax.experimental.pallas import tpu as pltpu
from jax.sharding import PartitionSpec as P

fresnel_scale = 4
LANE = 128
SUB = 8
TOP = 32767.0
VMEM_LIMIT = 56 * 1024 * 1024


def split_table(table):
    high = table.astype(ml_dtypes.bfloat16)
    low = (table - high.astype(np.float32)).astype(ml_dtypes.bfloat16)
    return high, low


def dft_tables(size):
    index = np.arange(size)
    angle = 2.0 * math.pi / size * ((index[:, None] * index[None, :]) % size)
    re = np.cos(angle) / math.sqrt(size)
    im = -np.sin(angle) / math.sqrt(size)
    table = np.block([[re, im], [-im, re]]).astype(np.float32)
    return split_table(table), split_table(np.ascontiguousarray(table.T))


def chirp_vectors(size):
    index = np.arange(size)
    phase = (index - size // 2) ** 2 % (2 * fresnel_scale * size)
    angle = math.pi / (fresnel_scale * size) * phase
    return np.cos(angle).astype(np.float32), np.sin(angle).astype(np.float32)


def halves(x):
    high = x.astype(jnp.bfloat16)
    return high, (x - high.astype(jnp.float32)).astype(jnp.bfloat16)


def dot(a, b):
    return jnp.dot(a, b, preferred_element_type=jnp.float32)


def right_mix(x, high, low):
    x_high, x_low = halves(x)
    return dot(x_high, high[...]) + (dot(x_low, high[...]) + dot(x_high, low[...]))


def left_mix(high, low, x):
    x_high, x_low = halves(x)
    return dot(high[...], x_high) + (dot(high[...], x_low) + dot(low[...], x_high))


def factor_kernel(pos, rows, size, start, probe, row_cos, row_sin, col, chirp, pc, doubled):
    doubled[:, :size] = probe[...].astype(jnp.float32)
    doubled[:, size : 2 * size] = doubled[:, :size]
    doubled[:, 2 * size :] = jnp.zeros_like(doubled[:, 2 * size :])
    cc, cs = col[0:1, :], col[1:2, :]
    for p in range(pos):
        here = pl.ds(pl.multiple_of(start[p] // SUB * SUB, SUB), rows + SUB)
        turn = (rows + SUB - start[p] % SUB) % (rows + SUB)
        rc = pltpu.roll(row_cos[here, :], turn, 0)[:rows, 0:1]
        rs = pltpu.roll(row_sin[here, :], turn, 0)[:rows, 0:1]
        ch_re = rc * cc - rs * cs
        ch_im = rs * cc + rc * cs
        pr_re = pltpu.roll(doubled[0, here, :], turn, 0)[:rows]
        pr_im = pltpu.roll(doubled[1, here, :], turn, 0)[:rows]
        chirp[p, 0] = ch_re
        chirp[p, 1] = ch_im
        pc[p, 0] = pr_re * ch_re - pr_im * ch_im
        pc[p, 1] = pr_re * ch_im + pr_im * ch_re


def forward_kernel(pos, rows, size, depth, meta, band, pc, high, low, half, patch, psi):
    width = band.shape[2]
    span = size + LANE
    ids = lax.broadcasted_iota(jnp.int32, (rows, size), 0)
    for p in range(pos):
        first, second, left, cut = meta[p, 0], meta[p, 1], meta[p, 2], meta[p, 3]
        base = pl.multiple_of(jnp.minimum(left // LANE * LANE, width - span), LANE)
        turn = (span - (left - base)) % span
        for part in range(2):
            def tile(cycle):
                at = pl.multiple_of(cycle * rows, rows)
                raw = band[part, pl.ds(at, rows), pl.ds(base, span)].astype(jnp.float32)
                return pltpu.roll(raw, turn, 1)[:, :size]

            patch[p, part] = jnp.where(ids >= cut, tile(first), tile(second))
        o_re, o_im = patch[p, 0], patch[p, 1]
        here = pl.ds(p * rows, rows)
        psi[here, :size] = o_re * pc[p, 0] - o_im * pc[p, 1]
        psi[here, size:] = o_re * pc[p, 1] + o_im * pc[p, 0]
    out = right_mix(psi[...], high, low)
    block = size // depth
    for d in range(depth):
        for part in range(2):
            for p in range(pos):
                half[d, part, p] = out[
                    p * rows : (p + 1) * rows, part * size + d * block : part * size + (d + 1) * block
                ]


def middle_kernel(pos, rows, size, depth, half, data, fwd_high, fwd_low, inv_high, inv_low, mid, stack):
    block = size // depth
    for d in range(depth):
        for part in range(2):
            for p in range(pos):
                stack[part * size + d * rows : part * size + (d + 1) * rows,
                      p * block : (p + 1) * block] = half[d, part, p]
    far = left_mix(fwd_high, fwd_low, stack[...])
    re, im = far[:size], far[size:]
    excess = re * re + im * im - data[...]
    stack[:size] = excess * re
    stack[size:] = excess * im
    out = left_mix(inv_high, inv_low, stack[...])
    for d in range(depth):
        for part in range(2):
            for p in range(pos):
                mid[d, part, p] = out[part * size + d * rows : part * size + (d + 1) * rows,
                                      p * block : (p + 1) * block]


def turn_column(column, rows):
    eye = lax.broadcasted_iota(jnp.int32, (rows, rows), 0) == lax.broadcasted_iota(
        jnp.int32, (rows, rows), 1
    )
    return jnp.sum(jnp.where(eye, column, 0.0), axis=0, keepdims=True)


def turn_row(row, rows):
    eye = lax.broadcasted_iota(jnp.int32, (rows, rows), 0) == lax.broadcasted_iota(
        jnp.int32, (rows, rows), 1
    )
    return jnp.sum(jnp.where(eye, row, 0.0), axis=1, keepdims=True)


def backward_kernel(
    pos, rows, size, depth, start, mid, patch, pc, chirp, high, low, codes, scales, probe, stack, doubled
):
    block = size // depth
    for d in range(depth):
        for part in range(2):
            for p in range(pos):
                stack[p * rows : (p + 1) * rows,
                      part * size + d * block : part * size + (d + 1) * block] = mid[d, part, p]
    back = right_mix(stack[...], high, low)
    doubled[...] = jnp.zeros_like(doubled)
    for p in range(pos):
        b_re = back[p * rows : (p + 1) * rows, :size]
        b_im = back[p * rows : (p + 1) * rows, size:]
        c_re = pc[p, 0] * b_re + pc[p, 1] * b_im
        c_im = pc[p, 0] * b_im - pc[p, 1] * b_re
        for part, value in enumerate((c_re, c_im)):
            for b in range(size // LANE):
                lanes = slice(b * LANE, (b + 1) * LANE)
                piece = value[:, lanes]
                peak = jnp.max(jnp.abs(piece), axis=1, keepdims=True)
                safe = jnp.where(peak > 1e-30, peak, 1.0)
                coded = jnp.round(piece * (TOP / safe)).astype(jnp.int32)
                codes[p, part, :, lanes] = coded.astype(jnp.int16)
                scales[p, part, b : b + 1, :] = turn_column(safe * (1.0 / TOP), rows)
        g_re = b_re * chirp[p, 0] + b_im * chirp[p, 1]
        g_im = b_im * chirp[p, 0] - b_re * chirp[p, 1]
        o_re, o_im = patch[p, 0], patch[p, 1]
        here = pl.ds(pl.multiple_of(start[p] // SUB * SUB, SUB), rows + SUB)
        margin = jnp.zeros((SUB, size), jnp.float32)
        for part, value in enumerate((o_re * g_re + o_im * g_im, o_re * g_im - o_im * g_re)):
            tall = jnp.concatenate([value, margin], axis=0)
            doubled[part, here, :] += pltpu.roll(tall, start[p] % SUB, 0)
    probe[...] = doubled[:, :size] + doubled[:, size : 2 * size]


def place_kernel(groups, pos, rows, size, cols, meta, codes, scales, grad):
    grad[...] = jnp.zeros_like(grad)
    row_ids = lax.broadcasted_iota(jnp.int32, (rows, cols), 0)
    col_ids = lax.broadcasted_iota(jnp.int32, (rows, cols), 1)

    def slot(q, carry):
        g, p = q // pos, q % pos
        first, second, shift, cut = meta[q, 0], meta[q, 1], meta[q, 2], meta[q, 3]

        @pl.when(jnp.logical_and(shift > -cols, shift < size))
        def _():
            turn = (size - shift) % size
            inside = jnp.logical_and(col_ids + shift >= 0, col_ids + shift < size)
            take = row_ids >= cut
            for part in range(2):
                pieces = []
                for b in range(size // LANE):
                    raw = codes[g, p, part, :, b * LANE : (b + 1) * LANE].astype(jnp.int32)
                    unit = turn_row(scales[g, p, part, b : b + 1, :], rows)
                    pieces.append(raw.astype(jnp.float32) * unit)
                value = pltpu.roll(jnp.concatenate(pieces, axis=1), turn, 1)[:, :cols]
                value = jnp.where(inside, value, 0.0)
                grad[part, first] += jnp.where(take, value, 0.0)
                grad[part, second] += jnp.where(take, 0.0, value)

        return carry

    lax.fori_loop(0, groups * pos, slot, 0)


def call(kernel, outs, specs, scratch=(), flops=0, moved=0):
    return pl.pallas_call(
        kernel,
        out_shape=outs,
        in_specs=specs,
        out_specs=jax.tree.map(lambda _: pl.BlockSpec(memory_space=pltpu.VMEM), outs),
        scratch_shapes=list(scratch),
        compiler_params=pltpu.CompilerParams(vmem_limit_bytes=VMEM_LIMIT),
        cost_estimate=pl.CostEstimate(flops=flops, bytes_accessed=moved, transcendentals=0),
    )


def on_device(scan_size, depth_size, object_slice, probe_field, offsets, assignment, intensities):
    depth_index = lax.axis_index("depth")
    scan_index = lax.axis_index("scan")
    _, cycles, rows, cols = object_slice.shape
    size = probe_field.shape[2]
    pos = assignment.shape[0]
    block = size // depth_size
    f32 = jnp.float32
    vm = pl.BlockSpec(memory_space=pltpu.VMEM)
    sm = pl.BlockSpec(memory_space=pltpu.SMEM)
    (t_high, t_low), (u_high, u_low) = dft_tables(size)
    ch_cos, ch_sin = chirp_vectors(size)

    band = lax.all_gather(object_slice, "scan", axis=3, tiled=True)
    full = band.shape[3]
    band = band.reshape(2, cycles * rows, full)
    slots = lax.all_gather(assignment, "scan", axis=0, tiled=True)

    def describe(where):
        top, left = where[:, 0], where[:, 1]
        first = top // size
        second = jnp.minimum(first + 1, cycles - 1)
        cut = top % size - depth_index * rows
        return jnp.stack([first, second, left, cut], 1).astype(jnp.int32), top

    meta, top = describe(offsets[assignment])
    start = (depth_index * rows - top) % size
    meta_all, _ = describe(offsets[slots])
    meta_all = jnp.stack(
        [meta_all[:, 0], meta_all[:, 1], scan_index * cols - meta_all[:, 2], meta_all[:, 3]], 1
    )

    wide = jax.ShapeDtypeStruct((pos, 2, rows, size), f32)
    cut_shape = jax.ShapeDtypeStruct((depth_size, 2, pos, rows, block), f32)
    row_cos = np.ascontiguousarray(np.broadcast_to(np.resize(ch_cos, 2 * size + SUB)[:, None], (2 * size + SUB, LANE)))
    row_sin = np.ascontiguousarray(np.broadcast_to(np.resize(ch_sin, 2 * size + SUB)[:, None], (2 * size + SUB, LANE)))
    chirp, pc = call(
        functools.partial(factor_kernel, pos, rows, size),
        (wide, wide),
        [sm, vm, vm, vm, vm],
        [pltpu.VMEM((2, 2 * size + SUB, size), f32)],
        flops=10_000_000,
        moved=4_000_000,
    )(start, probe_field, row_cos, row_sin, np.stack([ch_cos, ch_sin]))
    data = intensities.transpose(2, 0, 1).reshape(size, pos * block)

    half, patch = call(
        functools.partial(forward_kernel, pos, rows, size, depth_size),
        (cut_shape, wide),
        [sm, vm, vm, vm, vm],
        [pltpu.VMEM((pos * rows, 2 * size), f32)],
    )(meta, band, pc, t_high, t_low)
    half = lax.all_to_all(half, "depth", split_axis=0, concat_axis=0, tiled=True)
    mid = call(
        functools.partial(middle_kernel, pos, rows, size, depth_size),
        cut_shape,
        [vm] * 6,
        [pltpu.VMEM((2 * size, pos * block), f32)],
    )(half, data, u_high, u_low, t_high, t_low)
    mid = lax.all_to_all(mid, "depth", split_axis=0, concat_axis=0, tiled=True)
    codes, scales, probe = call(
        functools.partial(backward_kernel, pos, rows, size, depth_size),
        (
            jax.ShapeDtypeStruct((pos, 2, rows, size), jnp.int16),
            jax.ShapeDtypeStruct((pos, 2, size // LANE, rows), f32),
            jax.ShapeDtypeStruct((2, size, size), f32),
        ),
        [sm, vm, vm, vm, vm, vm, vm],
        [pltpu.VMEM((pos * rows, 2 * size), f32), pltpu.VMEM((2, 2 * size + SUB, size), f32)],
    )(start, mid, patch, pc, chirp, u_high, u_low)

    all_codes = lax.all_gather(codes, "scan", axis=0, tiled=False)
    all_scales = lax.all_gather(scales, "scan", axis=0, tiled=False)
    probe_part = lax.psum_scatter(probe, "depth", scatter_dimension=1, tiled=True)
    probe_grad = lax.psum(probe_part, "scan") * (pos * scan_size) ** (-0.5)
    object_grad = call(
        functools.partial(place_kernel, scan_size, pos, rows, size, cols),
        jax.ShapeDtypeStruct((2, cycles, rows, cols), f32),
        [sm, vm, vm],
    )(meta_all, all_codes, all_scales)
    return object_grad, probe_grad


def solution(mesh):
    return jax.shard_map(
        functools.partial(on_device, mesh.shape["scan"], mesh.shape["depth"]),
        mesh=mesh,
        in_specs=(P(None, None, "depth", "scan"), P(), P(), P("scan"), P("scan", "depth", None)),
        out_specs=(P(None, None, "depth", "scan"), P(None, "depth", None)),
        check_vma=False,
    )
```

```python
import functools
import math

import jax
import jax.numpy as jnp
import ml_dtypes
import numpy as np
from jax import lax
from jax.experimental import pallas as pl
from jax.experimental.pallas import tpu as pltpu
from jax.sharding import PartitionSpec as P

fresnel_scale = 4
LANE = 128
SUB = 8
TOP = 32767.0
VMEM_LIMIT = 56 * 1024 * 1024


def split_table(table):
    high = table.astype(ml_dtypes.bfloat16)
    low = (table - high.astype(np.float32)).astype(ml_dtypes.bfloat16)
    return high, low


def dft_tables(size, depth):
    index = np.arange(size)
    angle = 2.0 * math.pi / size * ((index[:, None] * index[None, :]) % size)
    re = np.cos(angle) / math.sqrt(size)
    im = -np.sin(angle) / math.sqrt(size)
    table = np.block([[re, im], [-im, re]]).astype(np.float32)
    by_row = table.reshape(2, depth, size // depth, 2 * size).transpose(1, 0, 2, 3)
    by_row = by_row.reshape(depth, 2 * size // depth, 2 * size)
    by_col = table.reshape(2 * size, 2, depth, size // depth).transpose(2, 0, 1, 3)
    by_col = by_col.reshape(depth, 2 * size, 2 * size // depth)
    return split_table(np.ascontiguousarray(by_row)), split_table(np.ascontiguousarray(by_col))


def chirp_vectors(size):
    index = np.arange(size)
    phase = (index - size // 2) ** 2 % (2 * fresnel_scale * size)
    angle = math.pi / (fresnel_scale * size) * phase
    return np.cos(angle).astype(np.float32), np.sin(angle).astype(np.float32)


def halves(x):
    high = x.astype(jnp.bfloat16)
    return high, (x - high.astype(jnp.float32)).astype(jnp.bfloat16)


def dot(a, b):
    return jnp.dot(a, b, preferred_element_type=jnp.float32)


def right_mix(x, high, low):
    x_high, x_low = halves(x)
    return dot(x_high, high) + (dot(x_low, high) + dot(x_high, low))


def left_mix(high, low, x):
    x_high, x_low = halves(x)
    return dot(high, x_high) + (dot(high, x_low) + dot(low, x_high))


MESH = pl.DeviceIdType.MESH


def send(src, dst, send_sem, recv_sem, axis, target):
    return pltpu.make_async_remote_copy(
        src_ref=src, dst_ref=dst, send_sem=send_sem, recv_sem=recv_sem,
        device_id={axis: target}, device_id_type=MESH,
    )


class Gather:
    def __init__(self, scan, pairs, sems):
        self.scan, self.chips = scan, scan // 2
        self.me = lax.axis_index("scan")
        self.chip, self.core = self.me // 2, self.me % 2
        self.other = self.me + 1 - 2 * self.core
        self.pairs = pairs
        self.up_sem, self.down_sem, self.side_sem, self.recv_sem, self.own_sem = sems

    def has(self, shift):
        return jnp.logical_and(self.chip + shift >= 0, self.chip + shift < self.chips)

    def greet(self, barrier):
        for shift in (-1, 1):
            @pl.when(self.has(shift))
            def _():
                pl.semaphore_signal(
                    barrier, inc=1, device_id={"scan": self.me + 2 * shift}, device_id_type=MESH
                )
        pl.semaphore_signal(barrier, inc=1, device_id={"scan": self.other}, device_id_type=MESH)
        ends = jnp.where(self.chip == 0, 1, 0) + jnp.where(self.chip == self.chips - 1, 1, 0)
        return 3 - ends

    def moves(self, block, way, source=None):
        sem, target = {
            "up": (self.up_sem, self.me + 2),
            "down": (self.down_sem, self.me - 2),
            "side": (self.side_sem, self.other),
        }[way]
        return [
            send(out.at[block] if source is None else source[i], out.at[block],
                 sem.at[i, block], self.recv_sem.at[i, block], "scan", target)
            for i, (_, out) in enumerate(self.pairs)
        ]

    def start(self):
        own = [ref for ref, _ in self.pairs]
        for shift, way in ((1, "up"), (-1, "down")):
            @pl.when(self.has(shift))
            def _():
                for move in self.moves(self.me, way, own):
                    move.start()
        for move in self.moves(self.me, "side", own):
            move.start()
        for i, (ref, out) in enumerate(self.pairs):
            pltpu.make_async_copy(ref, out.at[self.me], self.own_sem.at[i]).start()

    def step(self, t):
        for shift, way in ((-1, "up"), (1, "down")):
            @pl.when(self.has(shift * t))
            def _():
                block = self.me + 2 * shift * t
                for move in self.moves(block, "side"):
                    move.wait_recv()

                @pl.when(self.has(-shift))
                def _():
                    for move in self.moves(block, way):
                        move.start()

                for move in self.moves(block, "side"):
                    move.start()

    def finish(self):
        for t in range(self.chips):
            for shift in (-1, 1) if t else (0,):
                @pl.when(self.has(shift * t))
                def _():
                    block = self.other + 2 * shift * t
                    for move in self.moves(block, "side"):
                        move.wait_recv()
                    mine = self.me + 2 * shift * t
                    for move in self.moves(mine, "side"):
                        move.wait_send()
        for i, (ref, out) in enumerate(self.pairs):
            pltpu.make_async_copy(ref, out.at[self.me], self.own_sem.at[i]).wait()
        for shift, way in ((-1, "up"), (1, "down")):
            @pl.when(self.has(-shift))
            def _():
                for t in range(self.chips):
                    @pl.when(self.has(shift * t))
                    def _():
                        for move in self.moves(self.me + 2 * shift * t, way):
                            move.wait_send()


def gather_sems(scan, count):
    dma = pltpu.SemaphoreType.DMA
    return [dma((count, scan))] * 4 + [dma((count,))]


def band_kernel(scan, block, band, *sems):
    gather = Gather(scan, [(block, band)], sems)
    barrier = pltpu.get_barrier_semaphore()
    pl.semaphore_wait(barrier, gather.greet(barrier))
    gather.start()
    for t in range(1, gather.chips):
        gather.step(t)
    gather.finish()


def tail_kernel(
    scan, depth, block, codes, aux, probe, all_codes, all_aux, result,
    land, acc, near, below, above, up_out, down_out, final, *sems
):
    gather = Gather(scan, [(codes, all_codes), (aux, all_aux)], sems[:5])
    d_send, d_recv, near_sem, up_sem, down_sem, final_sem = sems[5:]
    me = lax.axis_index("depth")
    barrier = pltpu.get_barrier_semaphore()
    partners = [lax.rem(me + i, depth) for i in range(1, depth)]
    sources = [lax.rem(me + depth - i, depth) for i in range(1, depth)]
    for e in partners:
        pl.semaphore_signal(barrier, inc=1, device_id={"depth": e}, device_id_type=MESH)
    pl.semaphore_wait(barrier, gather.greet(barrier) + (depth - 1))
    gather.start()
    parts = [send(probe.at[e], land.at[me], d_send.at[e], d_recv.at[me], "depth", e) for e in partners]
    for copy in parts:
        copy.start()
    gather.step(1)
    total = probe[me]
    for e in sources:
        send(probe.at[e], land.at[e], d_send.at[e], d_recv.at[e], "depth", e).wait_recv()
        total = total + land[e]
    acc[...] = total
    core = gather.core
    cross = send(acc.at[1 - core], near, near_sem.at[0], near_sem.at[1], "scan", gather.other)
    cross.start()
    for t in range(2, gather.chips - 1):
        gather.step(t)
    cross.wait_recv()
    up = send(up_out, below, up_sem.at[0], up_sem.at[1], "scan", gather.me + 2)
    down = send(down_out, above, down_sem.at[0], down_sem.at[1], "scan", gather.me - 2)
    mine = acc[core] + near[...]
    final[core] = mine
    up_out[...] = mine
    down_out[...] = mine

    @pl.when(gather.chip == 0)
    def _():
        up.start()

    @pl.when(gather.chip == gather.chips - 1)
    def _():
        down.start()

    def pass_up():
        @pl.when(gather.has(-1))
        def _():
            up.wait_recv()
            up_out[...] += below[...]
            final[core] += below[...]

            @pl.when(gather.has(1))
            def _():
                up.start()

    def pass_down():
        @pl.when(gather.has(1))
        def _():
            down.wait_recv()
            down_out[...] += above[...]
            final[core] += above[...]

            @pl.when(gather.has(-1))
            def _():
                down.start()

    low_half = 2 * gather.chip < gather.chips

    @pl.when(low_half)
    def _():
        pass_up()
        pass_down()

    @pl.when(jnp.logical_not(low_half))
    def _():
        pass_down()
        pass_up()

    last = send(final.at[core], final.at[core], final_sem.at[0], final_sem.at[1], "scan", gather.other)
    last.start()
    if gather.chips > 2:
        gather.step(gather.chips - 1)
    send(final.at[1 - core], final.at[1 - core], final_sem.at[0], final_sem.at[1], "scan",
         gather.other).wait_recv()
    result[...] = final[...]
    gather.finish()
    last.wait_send()
    cross.wait_send()
    for copy in parts:
        copy.wait_send()

    @pl.when(gather.has(1))
    def _():
        up.wait_send()

    @pl.when(gather.has(-1))
    def _():
        down.wait_send()


def wave_kernel(
    pos, rows, size, depth, psi, data, row_high, row_low, col_high, col_low, back,
    out1, land1, out2, land2, far, resid, send1, recv1, send2, recv2
):
    me = lax.axis_index("depth")
    block = size // depth
    partners = [lax.rem(me + i, depth) for i in range(1, depth)]
    sources = [lax.rem(me + depth - i, depth) for i in range(1, depth)]
    barrier = pltpu.get_barrier_semaphore()
    for e in partners:
        pl.semaphore_signal(barrier, inc=1, device_id={"depth": e}, device_id_type=MESH)
    pl.semaphore_wait(barrier, depth - 1)

    def to_rows(chunk, count, side):
        re = [chunk[p * count : (p + 1) * count, :side] for p in range(pos)]
        im = [-chunk[p * count : (p + 1) * count, side:] for p in range(pos)]
        return jnp.concatenate([jnp.concatenate(re, 1), jnp.concatenate(im, 1)], 0)

    def to_lanes(chunk, count, side):
        lines = [
            jnp.concatenate(
                [chunk[:count, p * side : (p + 1) * side], -chunk[count:, p * side : (p + 1) * side]], 1
            )
            for p in range(pos)
        ]
        return jnp.concatenate(lines, 0)

    wave_high, wave_low = halves(psi[...])

    def forward(e):
        high, low = col_high[e], col_low[e]
        return dot(wave_high, high) + (dot(wave_low, high) + dot(wave_high, low))

    copies = []
    for e in partners:
        out1[e] = forward(e)
        copy = send(out1.at[e], land1.at[me], send1.at[e], recv1.at[me], "depth", e)
        copy.start()
        copies.append(copy)
    far[...] = left_mix(col_high[me], col_low[me], to_rows(forward(me), rows, block))
    for e in sources:
        send(out1.at[e], land1.at[e], send1.at[e], recv1.at[e], "depth", e).wait_recv()
        far[...] += left_mix(col_high[e], col_low[e], to_rows(land1[e], rows, block))
    re, im = far[:size], far[size:]
    excess = re * re + im * im - data[...]
    resid[:size] = excess * re
    resid[size:] = -(excess * im)
    res_high, res_low = halves(resid[...])

    def middle(e):
        high, low = row_high[e], row_low[e]
        return dot(high, res_high) + (dot(high, res_low) + dot(low, res_high))

    for e in partners:
        out2[e] = middle(e)
        copy = send(out2.at[e], land2.at[me], send2.at[e], recv2.at[me], "depth", e)
        copy.start()
        copies.append(copy)
    back[...] = right_mix(to_lanes(middle(me), rows, block), row_high[me], row_low[me])
    for e in sources:
        send(out2.at[e], land2.at[e], send2.at[e], recv2.at[e], "depth", e).wait_recv()
        back[...] += right_mix(to_lanes(land2[e], rows, block), row_high[e], row_low[e])
    for copy in copies:
        copy.wait_send()


def factor_kernel(pos, rows, size, start, probe, row_cos, row_sin, col, chirp, pc, doubled):
    doubled[:, :size] = probe[...].astype(jnp.float32)
    doubled[:, size : 2 * size] = doubled[:, :size]
    doubled[:, 2 * size :] = jnp.zeros_like(doubled[:, 2 * size :])
    cc, cs = col[0:1, :], col[1:2, :]
    for p in range(pos):
        here = pl.ds(pl.multiple_of(start[p] // SUB * SUB, SUB), rows + SUB)
        turn = (rows + SUB - start[p] % SUB) % (rows + SUB)
        rc = pltpu.roll(row_cos[here, :], turn, 0)[:rows, 0:1]
        rs = pltpu.roll(row_sin[here, :], turn, 0)[:rows, 0:1]
        ch_re = rc * cc - rs * cs
        ch_im = rs * cc + rc * cs
        pr_re = pltpu.roll(doubled[0, here, :], turn, 0)[:rows]
        pr_im = pltpu.roll(doubled[1, here, :], turn, 0)[:rows]
        chirp[p, 0] = ch_re
        chirp[p, 1] = ch_im
        pc[p, 0] = pr_re * ch_re - pr_im * ch_im
        pc[p, 1] = pr_re * ch_im + pr_im * ch_re


def window_kernel(pos, rows, size, cols, scan, meta, band, pc, patch, psi):
    count = -(-(size + cols) // LANE) * LANE // cols
    span = count * cols
    ids = lax.broadcasted_iota(jnp.int32, (rows, size), 0)
    for p in range(pos):
        first, second, left, cut = meta[p, 0], meta[p, 1], meta[p, 2], meta[p, 3]
        turn = (span - left % cols) % span
        for part in range(2):
            def tile(cycle):
                raw = [
                    band[jnp.minimum(left // cols + i, scan - 1), part, cycle].astype(jnp.float32)
                    for i in range(count)
                ]
                return pltpu.roll(jnp.concatenate(raw, 1), turn, 1)[:, :size]

            patch[p, part] = jnp.where(ids >= cut, tile(first), tile(second))
        o_re, o_im = patch[p, 0], patch[p, 1]
        here = pl.ds(p * rows, rows)
        psi[here, :size] = o_re * pc[p, 0] - o_im * pc[p, 1]
        psi[here, size:] = o_re * pc[p, 1] + o_im * pc[p, 0]


def turn_column(column, rows):
    eye = lax.broadcasted_iota(jnp.int32, (rows, rows), 0) == lax.broadcasted_iota(
        jnp.int32, (rows, rows), 1
    )
    return jnp.sum(jnp.where(eye, column, 0.0), axis=0, keepdims=True)


def turn_row(row, rows):
    eye = lax.broadcasted_iota(jnp.int32, (rows, rows), 0) == lax.broadcasted_iota(
        jnp.int32, (rows, rows), 1
    )
    return jnp.sum(jnp.where(eye, row, 0.0), axis=1, keepdims=True)


def grad_kernel(
    pos, rows, size, depth, start, place, back, patch, pc, chirp, codes, aux, probe, doubled
):
    block = size // depth
    doubled[...] = jnp.zeros_like(doubled)
    for p in range(pos):
        b_re = back[p * rows : (p + 1) * rows, :size]
        b_im = -back[p * rows : (p + 1) * rows, size:]
        c_re = pc[p, 0] * b_re + pc[p, 1] * b_im
        c_im = pc[p, 0] * b_im - pc[p, 1] * b_re
        for part, value in enumerate((c_re, c_im)):
            for b in range(size // LANE):
                lanes = slice(b * LANE, (b + 1) * LANE)
                piece = value[:, lanes]
                peak = jnp.max(jnp.abs(piece), axis=1, keepdims=True)
                safe = jnp.where(peak > 1e-30, peak, 1.0)
                coded = jnp.round(piece * (TOP / safe)).astype(jnp.int32)
                codes[p, part, :, lanes] = coded.astype(jnp.int16)
                line = part * (size // LANE) + b
                aux[p, line : line + 1, :] = turn_column(safe * (1.0 / TOP), rows)
        lines = 2 * (size // LANE)
        aux[p, lines:, :] = jnp.zeros((SUB, rows), jnp.float32)
        for i in range(2):
            aux[p, lines + i : lines + i + 1, :] = jnp.full((1, rows), place[p, i], jnp.float32)
        g_re = b_re * chirp[p, 0] + b_im * chirp[p, 1]
        g_im = b_im * chirp[p, 0] - b_re * chirp[p, 1]
        o_re, o_im = patch[p, 0], patch[p, 1]
        here = pl.ds(pl.multiple_of(start[p] // SUB * SUB, SUB), rows + SUB)
        margin = jnp.zeros((SUB, size), jnp.float32)
        for part, value in enumerate((o_re * g_re + o_im * g_im, o_re * g_im - o_im * g_re)):
            tall = jnp.concatenate([value, margin], axis=0)
            doubled[part, here, :] += pltpu.roll(tall, start[p] % SUB, 0)
    for d in range(depth):
        low, high = d * block, (d + 1) * block
        probe[d] = doubled[:, low:high] + doubled[:, size + low : size + high]


def place_kernel(groups, pos, rows, size, cols, meta, codes, aux, grad):
    grad[...] = jnp.zeros_like(grad)
    row_ids = lax.broadcasted_iota(jnp.int32, (rows, cols), 0)
    col_ids = lax.broadcasted_iota(jnp.int32, (rows, cols), 1)

    def slot(q, carry):
        g, p = q // pos, q % pos
        first, second, shift, cut = meta[q, 0], meta[q, 1], meta[q, 2], meta[q, 3]

        @pl.when(jnp.logical_and(shift > -cols, shift < size))
        def _():
            turn = (size - shift) % size
            inside = jnp.logical_and(col_ids + shift >= 0, col_ids + shift < size)
            take = row_ids >= cut
            for part in range(2):
                pieces = []
                for b in range(size // LANE):
                    raw = codes[g, p, part, :, b * LANE : (b + 1) * LANE].astype(jnp.int32)
                    line = part * (size // LANE) + b
                    unit = turn_row(aux[g, p, line : line + 1, :], rows)
                    pieces.append(raw.astype(jnp.float32) * unit)
                value = pltpu.roll(jnp.concatenate(pieces, axis=1), turn, 1)[:, :cols]
                value = jnp.where(inside, value, 0.0)
                grad[part, first] += jnp.where(take, value, 0.0)
                grad[part, second] += jnp.where(take, 0.0, value)

        return carry

    lax.fori_loop(0, groups * pos, slot, 0)


def call(kernel, outs, specs, scratch=(), collective=None, out_specs=None):
    vm = pl.BlockSpec(memory_space=pltpu.VMEM)
    return pl.pallas_call(
        kernel,
        out_shape=outs,
        in_specs=specs,
        out_specs=out_specs or jax.tree.map(lambda _: vm, outs),
        scratch_shapes=list(scratch),
        compiler_params=pltpu.CompilerParams(
            vmem_limit_bytes=VMEM_LIMIT,
            collective_id=collective,
            has_side_effects=collective is not None,
        ),
    )


def on_device(scan_size, depth_size, object_slice, probe_field, offsets, assignment, intensities):
    depth_index = lax.axis_index("depth")
    scan_index = lax.axis_index("scan")
    _, cycles, rows, cols = object_slice.shape
    size = probe_field.shape[2]
    pos = assignment.shape[0]
    block = size // depth_size
    f32 = jnp.float32
    shape = jax.ShapeDtypeStruct
    vm = pl.BlockSpec(memory_space=pltpu.VMEM)
    sm = pl.BlockSpec(memory_space=pltpu.SMEM)
    hbm = pl.BlockSpec(memory_space=pl.ANY)
    dma = pltpu.SemaphoreType.DMA
    (row_high, row_low), (col_high, col_low) = dft_tables(size, depth_size)
    ch_cos, ch_sin = chirp_vectors(size)

    def describe(top, left):
        first = top // size
        second = jnp.minimum(first + 1, cycles - 1)
        cut = top % size - depth_index * rows
        return jnp.stack([first, second, left, cut], 1).astype(jnp.int32)

    place = offsets[assignment]
    top, left = place[:, 0], place[:, 1]
    meta = describe(top, left)
    start = (depth_index * rows - top) % size

    wide = shape((pos, 2, rows, size), f32)
    tall = 2 * size + SUB
    row_cos = np.ascontiguousarray(np.broadcast_to(np.resize(ch_cos, tall)[:, None], (tall, LANE)))
    row_sin = np.ascontiguousarray(np.broadcast_to(np.resize(ch_sin, tall)[:, None], (tall, LANE)))
    chirp, pc = call(
        functools.partial(factor_kernel, pos, rows, size),
        (wide, wide),
        [sm, vm, vm, vm, vm],
        [pltpu.VMEM((2, tall, size), f32)],
    )(start, probe_field, row_cos, row_sin, np.stack([ch_cos, ch_sin]))
    data = intensities.transpose(2, 0, 1).reshape(size, pos * block)

    band = call(
        functools.partial(band_kernel, scan_size),
        shape((scan_size,) + object_slice.shape, object_slice.dtype),
        [hbm],
        gather_sems(scan_size, 1),
        collective=0,
        out_specs=hbm,
    )(object_slice)
    patch, psi = call(
        functools.partial(window_kernel, pos, rows, size, cols, scan_size),
        (wide, shape((pos * rows, 2 * size), f32)),
        [sm, vm, vm],
    )(meta, band, pc)
    chunk = pltpu.VMEM((depth_size, pos * rows, 2 * block), f32)
    turned = pltpu.VMEM((depth_size, 2 * rows, pos * block), f32)
    tower = pltpu.VMEM((2 * size, pos * block), f32)
    back = call(
        functools.partial(wave_kernel, pos, rows, size, depth_size),
        shape((pos * rows, 2 * size), f32),
        [vm] * 6,
        [chunk, chunk, turned, turned, tower, tower] + [dma((depth_size,))] * 4,
        collective=1,
    )(psi, data, row_high, row_low, col_high, col_low)
    lines = 2 * (size // LANE) + SUB
    codes, aux, probe = call(
        functools.partial(grad_kernel, pos, rows, size, depth_size),
        (
            shape((pos, 2, rows, size), jnp.int16),
            shape((pos, lines, rows), f32),
            shape((depth_size, 2, block, size), f32),
        ),
        [sm, sm, vm, vm, vm, vm],
        [pltpu.VMEM((2, tall, size), f32)],
    )(start, place.astype(f32), back, patch, pc, chirp)
    slab = pltpu.VMEM((block, size), f32)
    pair = pltpu.VMEM((2, block, size), f32)
    all_codes, all_aux, probe_sum = call(
        functools.partial(tail_kernel, scan_size, depth_size, block),
        (
            shape((scan_size,) + codes.shape, codes.dtype),
            shape((scan_size,) + aux.shape, aux.dtype),
            shape((2, block, size), f32),
        ),
        [hbm, hbm, vm],
        [pltpu.VMEM((depth_size, 2, block, size), f32), pair, slab, slab, slab, slab, slab, pair]
        + gather_sems(scan_size, 2)
        + [dma((depth_size,))] * 2
        + [dma((2,))] * 4,
        collective=2,
        out_specs=(hbm, hbm, vm),
    )(codes, aux, probe)
    spots = all_aux[:, :, lines - SUB : lines - SUB + 2, 0].astype(jnp.int32).reshape(-1, 2)
    meta_all = describe(spots[:, 0], scan_index * cols - spots[:, 1])
    object_grad = call(
        functools.partial(place_kernel, scan_size, pos, rows, size, cols),
        shape((2, cycles, rows, cols), f32),
        [sm, vm, vm],
    )(meta_all, all_codes, all_aux)
    return object_grad, probe_sum * (pos * scan_size) ** (-0.5)


def solution(mesh):
    return jax.shard_map(
        functools.partial(on_device, mesh.shape["scan"], mesh.shape["depth"]),
        mesh=mesh,
        in_specs=(P(None, None, "depth", "scan"), P(), P(), P("scan"), P("scan", "depth", None)),
        out_specs=(P(None, None, "depth", "scan"), P(None, "depth", None)),
        check_vma=False,
    )
```

```python
import functools
import math

import jax
import jax.numpy as jnp
import ml_dtypes
import numpy as np
from jax import lax
from jax.experimental import pallas as pl
from jax.experimental.pallas import tpu as pltpu
from jax.sharding import PartitionSpec as P

fresnel_scale = 4
LANE = 128
SUB = 8
TOP = 32767.0
VMEM_LIMIT = 56 * 1024 * 1024


def split_table(table):
    high = table.astype(ml_dtypes.bfloat16)
    low = (table - high.astype(np.float32)).astype(ml_dtypes.bfloat16)
    return high, low


def dft_tables(size, depth):
    index = np.arange(size)
    angle = 2.0 * math.pi / size * ((index[:, None] * index[None, :]) % size)
    re = np.cos(angle) / math.sqrt(size)
    im = -np.sin(angle) / math.sqrt(size)
    table = np.block([[re, im], [-im, re]]).astype(np.float32)
    by_row = table.reshape(2, depth, size // depth, 2 * size).transpose(1, 0, 2, 3)
    by_row = by_row.reshape(depth, 2 * size // depth, 2 * size)
    by_col = table.reshape(2 * size, 2, depth, size // depth).transpose(2, 0, 1, 3)
    by_col = by_col.reshape(depth, 2 * size, 2 * size // depth)
    return split_table(np.ascontiguousarray(by_row)), split_table(np.ascontiguousarray(by_col))


def chirp_vectors(size):
    index = np.arange(size)
    phase = (index - size // 2) ** 2 % (2 * fresnel_scale * size)
    angle = math.pi / (fresnel_scale * size) * phase
    return np.cos(angle).astype(np.float32), np.sin(angle).astype(np.float32)


def halves(x):
    high = x.astype(jnp.bfloat16)
    return high, (x - high.astype(jnp.float32)).astype(jnp.bfloat16)


def dot(a, b):
    return jnp.dot(a, b, preferred_element_type=jnp.float32)


def right_mix(x, high, low):
    x_high, x_low = halves(x)
    return dot(x_high, high) + (dot(x_low, high) + dot(x_high, low))


def left_mix(high, low, x):
    x_high, x_low = halves(x)
    return dot(high, x_high) + (dot(high, x_low) + dot(low, x_high))


MESH = pl.DeviceIdType.MESH


def send(src, dst, send_sem, recv_sem, axis, target):
    return pltpu.make_async_remote_copy(
        src_ref=src, dst_ref=dst, send_sem=send_sem, recv_sem=recv_sem,
        device_id={axis: target}, device_id_type=MESH,
    )


class Gather:
    def __init__(self, scan, pairs, sems):
        self.scan, self.chips = scan, scan // 2
        self.me = lax.axis_index("scan")
        self.chip, self.core = self.me // 2, self.me % 2
        self.other = self.me + 1 - 2 * self.core
        self.pairs = pairs
        self.up_sem, self.down_sem, self.side_sem, self.recv_sem, self.own_sem = sems

    def has(self, shift):
        return jnp.logical_and(self.chip + shift >= 0, self.chip + shift < self.chips)

    def greet(self, barrier):
        for shift in (-1, 1):
            @pl.when(self.has(shift))
            def _():
                pl.semaphore_signal(
                    barrier, inc=1, device_id={"scan": self.me + 2 * shift}, device_id_type=MESH
                )
        pl.semaphore_signal(barrier, inc=1, device_id={"scan": self.other}, device_id_type=MESH)
        ends = jnp.where(self.chip == 0, 1, 0) + jnp.where(self.chip == self.chips - 1, 1, 0)
        return 3 - ends

    def moves(self, block, way, source=None):
        sem, target = {
            "up": (self.up_sem, self.me + 2),
            "down": (self.down_sem, self.me - 2),
            "side": (self.side_sem, self.other),
        }[way]
        return [
            send(out.at[block] if source is None else source[i], out.at[block],
                 sem.at[i, block], self.recv_sem.at[i, block], "scan", target)
            for i, (_, out) in enumerate(self.pairs)
        ]

    def start(self):
        own = [ref for ref, _ in self.pairs]
        for shift, way in ((1, "up"), (-1, "down")):
            @pl.when(self.has(shift))
            def _():
                for move in self.moves(self.me, way, own):
                    move.start()
        for move in self.moves(self.me, "side", own):
            move.start()
        for i, (ref, out) in enumerate(self.pairs):
            pltpu.make_async_copy(ref, out.at[self.me], self.own_sem.at[i]).start()

    def step(self, t):
        for shift, way in ((-1, "up"), (1, "down")):
            @pl.when(self.has(shift * t))
            def _():
                block = self.me + 2 * shift * t
                for move in self.moves(block, "side"):
                    move.wait_recv()

                @pl.when(self.has(-shift))
                def _():
                    for move in self.moves(block, way):
                        move.start()

                for move in self.moves(block, "side"):
                    move.start()

    def own_wait(self):
        for i, (ref, out) in enumerate(self.pairs):
            pltpu.make_async_copy(ref, out.at[self.me], self.own_sem.at[i]).wait()

    def side_wait(self, t, then=None):
        for shift in (-1, 1) if t else (0,):
            @pl.when(self.has(shift * t))
            def _():
                block = self.other + 2 * shift * t
                for move in self.moves(block, "side"):
                    move.wait_recv()
                if then is not None:
                    then(self.chip + shift * t)

    def finish(self):
        for t in range(self.chips):
            for shift in (-1, 1) if t else (0,):
                @pl.when(self.has(shift * t))
                def _():
                    for move in self.moves(self.me + 2 * shift * t, "side"):
                        move.wait_send()
        for shift, way in ((1, "up"), (-1, "down")):
            @pl.when(self.has(shift))
            def _():
                for t in range(self.chips):
                    @pl.when(self.has(-shift * t))
                    def _():
                        for move in self.moves(self.me - 2 * shift * t, way):
                            move.wait_send()


def gather_sems(scan, count):
    dma = pltpu.SemaphoreType.DMA
    return [dma((count, scan))] * 4 + [dma((count,))]


def probe_reduce(gather, me, probe, result, near, half, land, below, above, up_out, down_out, final, sems):
    near_sem, d_send, d_recv, up_sem, down_sem, final_sem = sems
    depth = half.shape[0]
    core = gather.core
    partners = [lax.rem(me + i, depth) for i in range(1, depth)]
    sources = [lax.rem(me + depth - i, depth) for i in range(1, depth)]
    cross = send(probe.at[1 - core], near, near_sem.at[0], near_sem.at[1], "scan", gather.other)
    cross.start()
    cross.wait_recv()
    half[...] = probe[core] + near[...]
    parts = [send(half.at[e], land.at[me], d_send.at[e], d_recv.at[me], "depth", e) for e in partners]
    for copy in parts:
        copy.start()
    gather.step(1)
    mine = half[me]
    for e in sources:
        send(half.at[e], land.at[e], d_send.at[e], d_recv.at[e], "depth", e).wait_recv()
        mine = mine + land[e]
    final[core] = mine
    up_out[...] = mine
    down_out[...] = mine
    up = send(up_out, below, up_sem.at[0], up_sem.at[1], "scan", gather.me + 2)
    down = send(down_out, above, down_sem.at[0], down_sem.at[1], "scan", gather.me - 2)

    @pl.when(gather.chip == 0)
    def _():
        up.start()

    @pl.when(gather.chip == gather.chips - 1)
    def _():
        down.start()

    for t in range(2, gather.chips - 1):
        gather.step(t)

    def pass_up():
        @pl.when(gather.has(-1))
        def _():
            up.wait_recv()
            up_out[...] += below[...]
            final[core] += below[...]

            @pl.when(gather.has(1))
            def _():
                up.start()

    def pass_down():
        @pl.when(gather.has(1))
        def _():
            down.wait_recv()
            down_out[...] += above[...]
            final[core] += above[...]

            @pl.when(gather.has(-1))
            def _():
                down.start()

    low_half = 2 * gather.chip < gather.chips

    @pl.when(low_half)
    def _():
        pass_up()
        pass_down()

    @pl.when(jnp.logical_not(low_half))
    def _():
        pass_down()
        pass_up()

    last = send(final.at[core], final.at[core], final_sem.at[0], final_sem.at[1], "scan", gather.other)
    last.start()
    if gather.chips > 2:
        gather.step(gather.chips - 1)
    send(final.at[1 - core], final.at[1 - core], final_sem.at[0], final_sem.at[1], "scan",
         gather.other).wait_recv()
    result[...] = final[...] * (gather.scan * gather.pos) ** (-0.5)
    last.wait_send()
    cross.wait_send()
    for copy in parts:
        copy.wait_send()

    @pl.when(gather.has(1))
    def _():
        up.wait_send()

    @pl.when(gather.has(-1))
    def _():
        down.wait_send()


def wave_part(
    me, pos, rows, size, depth, psi, data, row_high, row_low, col_high, col_low, back,
    out1, land1, out2, land2, far, resid, send1, recv1, send2, recv2
):
    block = size // depth
    partners = [lax.rem(me + i, depth) for i in range(1, depth)]
    sources = [lax.rem(me + depth - i, depth) for i in range(1, depth)]

    def to_rows(chunk, count, side):
        re = [chunk[p * count : (p + 1) * count, :side] for p in range(pos)]
        im = [-chunk[p * count : (p + 1) * count, side:] for p in range(pos)]
        return jnp.concatenate([jnp.concatenate(re, 1), jnp.concatenate(im, 1)], 0)

    def to_lanes(chunk, count, side):
        lines = [
            jnp.concatenate(
                [chunk[:count, p * side : (p + 1) * side], -chunk[count:, p * side : (p + 1) * side]], 1
            )
            for p in range(pos)
        ]
        return jnp.concatenate(lines, 0)

    wave_high, wave_low = halves(psi[...])

    def forward(e):
        high, low = col_high[e], col_low[e]
        return dot(wave_high, high) + (dot(wave_low, high) + dot(wave_high, low))

    copies = []
    for e in partners:
        out1[e] = forward(e)
        copy = send(out1.at[e], land1.at[me], send1.at[e], recv1.at[me], "depth", e)
        copy.start()
        copies.append(copy)
    far[...] = left_mix(col_high[me], col_low[me], to_rows(forward(me), rows, block))
    for e in sources:
        send(out1.at[e], land1.at[e], send1.at[e], recv1.at[e], "depth", e).wait_recv()
        far[...] += left_mix(col_high[e], col_low[e], to_rows(land1[e], rows, block))
    re, im = far[:size], far[size:]
    excess = re * re + im * im - data[...]
    resid[:size] = excess * re
    resid[size:] = -(excess * im)
    res_high, res_low = halves(resid[...])

    def middle(e):
        high, low = row_high[e], row_low[e]
        return dot(high, res_high) + (dot(high, res_low) + dot(low, res_high))

    for e in partners:
        out2[e] = middle(e)
        copy = send(out2.at[e], land2.at[me], send2.at[e], recv2.at[me], "depth", e)
        copy.start()
        copies.append(copy)
    back[...] = right_mix(to_lanes(middle(me), rows, block), row_high[me], row_low[me])
    for e in sources:
        send(out2.at[e], land2.at[e], send2.at[e], recv2.at[e], "depth", e).wait_recv()
        back[...] += right_mix(to_lanes(land2[e], rows, block), row_high[e], row_low[e])
    for copy in copies:
        copy.wait_send()


def wrap_hot(rows, size, start, axis):
    shape = (rows, size) if axis == 0 else (size, rows)
    spot = lax.broadcasted_iota(jnp.int32, shape, axis) + start
    spot = jnp.where(spot >= size, spot - size, spot)
    return spot == lax.broadcasted_iota(jnp.int32, shape, 1 - axis)


def as_ones(mask):
    return jnp.where(mask, 1.0, 0.0).astype(jnp.bfloat16)


def factor_part(pos, rows, size, start, probe, col, chirp, pc):
    cc, cs = col[0:1, :], col[1:2, :]
    for p in range(pos):
        hot = wrap_hot(rows, size, start[p], 0)
        rc = jnp.sum(jnp.where(hot, cc, 0.0), axis=1, keepdims=True)
        rs = jnp.sum(jnp.where(hot, cs, 0.0), axis=1, keepdims=True)
        ones = as_ones(hot)
        pr_re, pr_im = dot(ones, probe[0]), dot(ones, probe[1])
        ch_re = rc * cc - rs * cs
        ch_im = rs * cc + rc * cs
        chirp[p, 0] = ch_re
        chirp[p, 1] = ch_im
        pc[p, 0] = pr_re * ch_re - pr_im * ch_im
        pc[p, 1] = pr_re * ch_im + pr_im * ch_re


def window_add(pos, rows, size, cols, cycles, meta, band, patch, g):
    row_ids = lax.broadcasted_iota(jnp.int32, (rows, cols), 0)
    col_ids = lax.broadcasted_iota(jnp.int32, (cols, size), 0)
    out_ids = lax.broadcasted_iota(jnp.int32, (cols, size), 1)
    for p in range(pos):
        first, second, left, cut = meta[p]
        cycle = jnp.where(row_ids >= cut, first, second)
        picked = []
        for part in range(2):
            value = band[g, part, 0].astype(jnp.float32)
            for c in range(1, cycles):
                value = jnp.where(cycle == c, band[g, part, c].astype(jnp.float32), value)
            picked.append(value)
        ones = as_ones(col_ids + (g * cols - left) == out_ids)
        share = dot(jnp.concatenate(picked, 0).astype(jnp.bfloat16), ones)
        patch[p, 0] += share[:rows]
        patch[p, 1] += share[rows:]


def wave_start(pos, rows, size, patch, pc, psi):
    for p in range(pos):
        o_re, o_im = patch[p, 0], patch[p, 1]
        here = pl.ds(p * rows, rows)
        psi[here, :size] = o_re * pc[p, 0] - o_im * pc[p, 1]
        psi[here, size:] = o_re * pc[p, 1] + o_im * pc[p, 0]


def turn_column(column, rows):
    eye = lax.broadcasted_iota(jnp.int32, (rows, rows), 0) == lax.broadcasted_iota(
        jnp.int32, (rows, rows), 1
    )
    return jnp.sum(jnp.where(eye, column, 0.0), axis=0, keepdims=True)


def turn_row(row, rows):
    eye = lax.broadcasted_iota(jnp.int32, (rows, rows), 0) == lax.broadcasted_iota(
        jnp.int32, (rows, rows), 1
    )
    return jnp.sum(jnp.where(eye, row, 0.0), axis=1, keepdims=True)


def codes_part(pos, rows, size, place, back, pc, codes, aux):
    for p in range(pos):
        b_re = back[p * rows : (p + 1) * rows, :size]
        b_im = -back[p * rows : (p + 1) * rows, size:]
        c_re = pc[p, 0] * b_re + pc[p, 1] * b_im
        c_im = pc[p, 0] * b_im - pc[p, 1] * b_re
        for part, value in enumerate((c_re, c_im)):
            for b in range(size // LANE):
                lanes = slice(b * LANE, (b + 1) * LANE)
                piece = value[:, lanes]
                peak = jnp.max(jnp.abs(piece), axis=1, keepdims=True)
                safe = jnp.where(peak > 1e-30, peak, 1.0)
                coded = jnp.round(piece * (TOP / safe)).astype(jnp.int32)
                codes[p, part, :, lanes] = coded.astype(jnp.int16)
                line = part * (size // LANE) + b
                aux[p, line : line + 1, :] = turn_column(safe * (1.0 / TOP), rows)
        lines = 2 * (size // LANE)
        aux[p, lines:, :] = jnp.zeros((SUB, rows), jnp.float32)
        for i in range(2):
            aux[p, lines + i : lines + i + 1, :] = jnp.full((1, rows), place[p][i].astype(jnp.float32))


def terms_part(pos, rows, size, depth, start, back, patch, chirp, probe):
    block = size // depth
    ones, values = [], []
    for p in range(pos):
        b_re = back[p * rows : (p + 1) * rows, :size]
        b_im = -back[p * rows : (p + 1) * rows, size:]
        g_re = b_re * chirp[p, 0] + b_im * chirp[p, 1]
        g_im = b_im * chirp[p, 0] - b_re * chirp[p, 1]
        o_re, o_im = patch[p, 0], patch[p, 1]
        values.append(jnp.concatenate([o_re * g_re + o_im * g_im, o_re * g_im - o_im * g_re], 1))
        ones.append(as_ones(wrap_hot(rows, size, start[p], 1)))
    high, low = halves(jnp.concatenate(values, 0))
    hot = jnp.concatenate(ones, 1)
    for part in range(2):
        lanes = slice(part * size, (part + 1) * size)
        moved = dot(hot, high[:, lanes]) + dot(hot, low[:, lanes])
        for d in range(depth):
            probe[part, d] = moved[d * block : (d + 1) * block]


def main_kernel(
    scan, depth, cycles, cols, pos, rows, size,
    place_ref, slab, probe_field, col, intensities, row_h, row_l, col_h, col_l,
    all_codes, all_aux, result,
    band, row_high, row_low, col_high, col_low, chirp, pc, data, patch, psi, back,
    out1, land1, out2, land2, far, resid, codes, aux, probe,
    near, half, land, below, above, up_out, down_out, final, *sems
):
    me = lax.axis_index("depth")
    block = size // depth
    first_gather = Gather(scan, [(slab, band)], sems[:5])
    gather = Gather(scan, [(codes, all_codes), (aux, all_aux)], sems[5:10])
    gather.pos = pos
    send1, recv1, send2, recv2, table_sem = sems[10:15]
    barrier = pltpu.get_barrier_semaphore()
    for i in range(1, depth):
        pl.semaphore_signal(
            barrier, inc=1, device_id={"depth": lax.rem(me + i, depth)}, device_id_type=MESH
        )
    pl.semaphore_wait(barrier, first_gather.greet(barrier) + (depth - 1))
    first_gather.start()
    tables = [
        pltpu.make_async_copy(src, dst, table_sem.at[i])
        for i, (src, dst) in enumerate(
            ((col_h, col_high), (col_l, col_low), (row_h, row_high), (row_l, row_low))
        )
    ]
    for copy in tables:
        copy.start()
    place, meta, start = [], [], []
    for p in range(pos):
        top, left = place_ref[p, 0], place_ref[p, 1]
        first = sum(jnp.where(top >= c * size, 1, 0) for c in range(1, cycles))
        inner = top - first * size
        begin = me * rows - inner
        place.append((top, left))
        meta.append((first, jnp.minimum(first + 1, cycles - 1), left, inner - me * rows))
        start.append(jnp.where(begin < 0, begin + size, begin))
    factor_part(pos, rows, size, start, probe_field, col, chirp, pc)
    data[...] = jnp.concatenate([intensities[p].T for p in range(pos)], 1)
    for copy in tables:
        copy.wait()
    patch[...] = jnp.zeros_like(patch)

    def add_chip(chip):
        def one(core, carry):
            window_add(pos, rows, size, cols, cycles, meta, band, patch, 2 * chip + core)
            return carry

        lax.fori_loop(0, 2, one, 0)

    first_gather.own_wait()
    for t in range(1, first_gather.chips):
        first_gather.step(t)
        first_gather.side_wait(t - 1, add_chip)
    first_gather.side_wait(first_gather.chips - 1, add_chip)
    first_gather.finish()
    wave_start(pos, rows, size, patch, pc, psi)
    wave_part(
        me, pos, rows, size, depth, psi, data, row_high, row_low, col_high, col_low, back,
        out1, land1, out2, land2, far, resid, send1, recv1, send2, recv2
    )
    codes_part(pos, rows, size, place, back, pc, codes, aux)
    gather.start()
    terms_part(pos, rows, size, depth, start, back, patch, chirp, probe)
    probe_reduce(
        gather, me, probe, result, near, half, land, below, above, up_out, down_out, final, sems[15:]
    )
    gather.own_wait()
    for t in range(gather.chips):
        gather.side_wait(t)
    gather.finish()


def place_kernel(groups, pos, rows, size, cols, meta, codes, aux, grad):
    grad[...] = jnp.zeros_like(grad)
    row_ids = lax.broadcasted_iota(jnp.int32, (rows, cols), 0)
    col_ids = lax.broadcasted_iota(jnp.int32, (rows, cols), 1)

    def slot(q, carry):
        g, p = q // pos, q % pos
        first, second, shift, cut = meta[q, 0], meta[q, 1], meta[q, 2], meta[q, 3]

        @pl.when(jnp.logical_and(shift > -cols, shift < size))
        def _():
            turn = (size - shift) % size
            inside = jnp.logical_and(col_ids + shift >= 0, col_ids + shift < size)
            take = row_ids >= cut
            for part in range(2):
                pieces = []
                for b in range(size // LANE):
                    raw = codes[g, p, part, :, b * LANE : (b + 1) * LANE].astype(jnp.int32)
                    line = part * (size // LANE) + b
                    unit = turn_row(aux[g, p, line : line + 1, :], rows)
                    pieces.append(raw.astype(jnp.float32) * unit)
                value = pltpu.roll(jnp.concatenate(pieces, axis=1), turn, 1)[:, :cols]
                value = jnp.where(inside, value, 0.0)
                grad[part, first] += jnp.where(take, value, 0.0)
                grad[part, second] += jnp.where(take, 0.0, value)

        return carry

    lax.fori_loop(0, groups * pos, slot, 0)


def call(kernel, outs, specs, scratch=(), collective=None, out_specs=None):
    vm = pl.BlockSpec(memory_space=pltpu.VMEM)
    return pl.pallas_call(
        kernel,
        out_shape=outs,
        in_specs=specs,
        out_specs=out_specs or jax.tree.map(lambda _: vm, outs),
        scratch_shapes=list(scratch),
        compiler_params=pltpu.CompilerParams(
            vmem_limit_bytes=VMEM_LIMIT,
            collective_id=collective,
            has_side_effects=collective is not None,
        ),
    )


def on_device(scan_size, depth_size, object_slice, probe_field, offsets, assignment, intensities):
    depth_index = lax.axis_index("depth")
    scan_index = lax.axis_index("scan")
    _, cycles, rows, cols = object_slice.shape
    size = probe_field.shape[2]
    pos = assignment.shape[0]
    block = size // depth_size
    f32 = jnp.float32
    shape = jax.ShapeDtypeStruct
    vm = pl.BlockSpec(memory_space=pltpu.VMEM)
    sm = pl.BlockSpec(memory_space=pltpu.SMEM)
    hbm = pl.BlockSpec(memory_space=pl.ANY)
    dma = pltpu.SemaphoreType.DMA
    (row_high, row_low), (col_high, col_low) = dft_tables(size, depth_size)
    ch_cos, ch_sin = chirp_vectors(size)

    def describe(top, left):
        first = top // size
        second = jnp.minimum(first + 1, cycles - 1)
        cut = top % size - depth_index * rows
        return jnp.stack([first, second, left, cut], 1).astype(jnp.int32)

    lines = 2 * (size // LANE) + SUB
    wide = pltpu.VMEM((pos, 2, rows, size), f32)
    long = pltpu.VMEM((pos * rows, 2 * size), f32)
    chunk = pltpu.VMEM((depth_size, pos * rows, 2 * block), f32)
    turned = pltpu.VMEM((depth_size, 2 * rows, pos * block), f32)
    tower = pltpu.VMEM((2 * size, pos * block), f32)
    slab = pltpu.VMEM((block, size), f32)
    stack = pltpu.VMEM((depth_size, block, size), f32)
    pair = pltpu.VMEM((2, block, size), f32)
    by_row = pltpu.VMEM(row_high.shape, jnp.bfloat16)
    by_col = pltpu.VMEM(col_high.shape, jnp.bfloat16)
    all_codes, all_aux, probe_grad = call(
        functools.partial(
            main_kernel, scan_size, depth_size, cycles, cols, pos, rows, size
        ),
        (
            shape((scan_size, pos, 2, rows, size), jnp.int16),
            shape((scan_size, pos, lines, rows), f32),
            shape((2, block, size), f32),
        ),
        [sm, hbm, vm, vm, vm, hbm, hbm, hbm, hbm],
        [pltpu.VMEM((scan_size,) + object_slice.shape, object_slice.dtype)]
        + [by_row, by_row, by_col, by_col]
        + [wide, wide]
        + [pltpu.VMEM((size, pos * block), f32), wide, long, long]
        + [chunk, chunk, turned, turned, tower, tower]
        + [pltpu.VMEM((pos, 2, rows, size), jnp.int16), pltpu.VMEM((pos, lines, rows), f32)]
        + [pltpu.VMEM((2, depth_size, block, size), f32)]
        + [stack, stack, stack, slab, slab, slab, slab, pair]
        + gather_sems(scan_size, 1)
        + gather_sems(scan_size, 2)
        + [dma((depth_size,))] * 4
        + [dma((4,)), dma((2,)), dma((depth_size,)), dma((depth_size,)), dma((2,)), dma((2,)), dma((2,))],
        collective=0,
        out_specs=(hbm, hbm, vm),
    )(
        offsets[assignment], object_slice, probe_field, np.stack([ch_cos, ch_sin]),
        intensities, row_high, row_low, col_high, col_low,
    )
    spots = all_aux[:, :, lines - SUB : lines - SUB + 2, 0].astype(jnp.int32).reshape(-1, 2)
    meta_all = describe(spots[:, 0], scan_index * cols - spots[:, 1])
    object_grad = call(
        functools.partial(place_kernel, scan_size, pos, rows, size, cols),
        shape((2, cycles, rows, cols), f32),
        [sm, vm, vm],
    )(meta_all, all_codes, all_aux)
    return object_grad, probe_grad


def solution(mesh):
    return jax.shard_map(
        functools.partial(on_device, mesh.shape["scan"], mesh.shape["depth"]),
        mesh=mesh,
        in_specs=(P(None, None, "depth", "scan"), P(), P(), P("scan"), P("scan", "depth", None)),
        out_specs=(P(None, None, "depth", "scan"), P(None, "depth", None)),
        check_vma=False,
    )
```
